32 devices in a mesh: band: 4 (over x, core), col: 8 (over z, y).
Axes of the slice: x: 2, y: 2, z: 4, core: 2. Of those that a mesh axis runs over, the one named last changes fastest.
Arguments:
- series: float32 [16, 8192], P(None, ('band', 'col')), may hold values from -6 to 6
- tail: float32 [16, 255], replicated, may hold values from -6 to 6
Outputs:
- profile: float32 [16, 8192], P(None, ('band', 'col'))
The draws below stay inside these ranges and needn't reach their ends.
All inputs are finite; a program needn't handle non-finite values.
Results may differ from the reference program's by a relative error of at most 0.0003.
Values may be sent and summed in bfloat16 or wider, within the bound.
A program may use at most 64 MiB of HBM per device.

```python
import jax
import jax.numpy as jnp
from jax import lax

M = 256
CH = 16
TB = 256
KD = 4
EXCL = 64
NSUB = 8192
N_BAND = 4
N_COL = 8


def steps_of(own_key, shape, cuts, least, high):
    def one(axis_at, blocks):
        heights = jax.random.uniform(jax.random.fold_in(jax.random.fold_in(own_key, 6), axis_at), (blocks,), jnp.float32, least / len(cuts), high / len(cuts))
        return jnp.repeat(jnp.exp(heights), shape[axis_at] // blocks).reshape((-1,) + (1,) * (len(shape) - axis_at - 1))

    level = one(*cuts[0])
    for cut in cuts[1:]:
        level = level * one(*cut)
    return level


def scatter_about(key, dims, scale, most, cuts=(), held_as=jnp.bfloat16):
    drawn = jax.random.normal(key, dims, jnp.float32) * scale
    if len(cuts) > 0:
        drawn = steps_of(key, dims, cuts, -0.22, 0.18) * drawn
    return jnp.clip(drawn, min=-most, max=most).astype(held_as)


def setup_inputs(seed: int = 0) -> dict:
    key_of = jax.random.split(jax.random.key(seed), 3)
    return {
        "series": scatter_about(key_of[0], (CH, NSUB), 1.0, 6.0, ((1, 32),), jnp.float32),
        "tail": scatter_about(key_of[1], (CH, M - 1), 1.0, 6.0, (), jnp.float32),
    }


epsilon = 1e-06

def normalize(samples, row_count, sub_length):
    window_index = jnp.arange(row_count, dtype=jnp.int32)[:, None] + jnp.arange(sub_length, dtype=jnp.int32)[None, :]
    windows = samples[window_index]
    average = lax.optimization_barrier(jnp.mean(windows, axis=1, keepdims=True))
    deviation = windows - average
    variance = lax.optimization_barrier(jnp.mean(deviation * deviation, axis=1, keepdims=True))
    return (deviation * lax.rsqrt(variance + epsilon)).astype(jnp.bfloat16)

def single_series(series_row, tail_row):
    devices = N_BAND * N_COL
    padded = jnp.concatenate([series_row, tail_row, jnp.zeros((KD * TB,), series_row.dtype)])
    offsets = jnp.arange(TB, dtype=jnp.int32)

    def visit(position, best_corr):
        position = jnp.asarray(position).astype(jnp.int32)
        start = (position * TB).astype(jnp.int32)
        own_rows = normalize(lax.dynamic_slice_in_dim(padded, start, TB + M - 1), TB, M).astype(jnp.float32)
        for offset in range(KD):
            other = normalize(lax.dynamic_slice_in_dim(padded, start + offset * TB, TB + M - 1), TB, M).astype(jnp.float32)
            scores = jnp.dot(own_rows, other.T, precision=lax.Precision.HIGHEST, preferred_element_type=jnp.float32) / M
            lag_grid = offset * TB + offsets[None, :] - offsets[:, None]
            valid = (jnp.abs(lag_grid) >= EXCL) & (position + offset < devices)
            scores = jnp.where(valid, scores, -4.0)
            row_best = lax.optimization_barrier(jnp.max(scores, axis=1))
            col_best = lax.optimization_barrier(jnp.max(scores, axis=0))
            current = lax.dynamic_slice_in_dim(best_corr, start, TB)
            best_corr = lax.dynamic_update_slice_in_dim(best_corr, jnp.maximum(current, row_best), start, 0)
            target = (jnp.minimum(position + offset, devices - 1) * TB).astype(jnp.int32)
            current = lax.dynamic_slice_in_dim(best_corr, target, TB)
            best_corr = lax.dynamic_update_slice_in_dim(best_corr, jnp.maximum(current, col_best), target, 0)
        return best_corr
    best_corr = lax.fori_loop(0, devices, visit, jnp.full((NSUB,), -4.0, series_row.dtype))
    return jnp.sqrt(2.0 * M * (1.0 - best_corr))

def reference(series, tail):
    return lax.map(lambda pair: single_series(pair[0], pair[1]), (series, tail))
```

```python
import functools

import jax
import jax.numpy as jnp
from jax import lax
from jax.experimental import pallas as pl
from jax.experimental.pallas import tpu as pltpu
from jax.sharding import PartitionSpec as P

KD = 4
LANES = 128
SUBLANES = 8

epsilon = 1e-06

ORDER = (1, 2, -1, 3, -2, 4, -3)


def window_stats(samples, length):
    width = samples.shape[1]
    mean, spread = samples, None
    count = 1
    while count < length:
        other = pltpu.roll(mean, width - count, 1)
        gap = mean - other
        term = gap * gap * (0.5 * count)
        if spread is None:
            spread = term
        else:
            spread = spread + pltpu.roll(spread, width - count, 1) + term
        mean = (mean + other) * 0.5
        count *= 2
    return mean, lax.rsqrt(spread * (1.0 / length) + epsilon)


def kernel(
    n_col,
    device_count,
    series_ref,
    tail_ref,
    out_ref,
    xs,
    mean_ref,
    scale_ref,
    bias_ref,
    next_bias_ref,
    prev_bias_ref,
    z_even,
    z_odd,
    local_sem,
    send_sem,
    recv_sem,
):
    channels, rows = series_ref.shape
    length = tail_ref.shape[1] + 1
    halves = length // LANES
    exclusion = length // 4
    width = xs.shape[1]
    before = KD - 1
    tiles = 2 * KD - 1
    position = lax.axis_index("band") * n_col + lax.axis_index("col")

    def device(index):
        return {"band": index // n_col, "col": lax.rem(index, n_col)}

    def inside(index):
        return (index >= 0) & (index < device_count)

    barrier = pltpu.get_barrier_semaphore()
    for offset in ORDER:
        source = position + offset

        @pl.when(inside(source))
        def _():
            pl.semaphore_signal(
                barrier, inc=1, device_id=device(source), device_id_type=pl.DeviceIdType.MESH
            )

    def place(offset):
        return xs.at[:, pl.ds((before + offset) * rows, rows)]

    local = pltpu.make_async_copy(series_ref, place(0), local_sem)
    local.start()

    for offset in range(1, KD + 1):

        @pl.when(position + offset == device_count)
        def _():
            start = (before + offset) * rows
            xs[:, start : start + length - 1] = tail_ref[...]

    row_at = lax.broadcasted_iota(jnp.int32, (rows, rows), 0)
    col_at = lax.broadcasted_iota(jnp.int32, (rows, rows), 1)
    away = -16.0 * length
    bias_ref[...] = jnp.where(jnp.abs(row_at - col_at) >= exclusion, 0.0, away)
    row_at = lax.broadcasted_iota(jnp.int32, (exclusion, LANES), 0)
    col_at = lax.broadcasted_iota(jnp.int32, (exclusion, LANES), 1)
    next_bias_ref[...] = jnp.where(col_at >= row_at, 0.0, away)
    prev_bias_ref[...] = jnp.where(LANES - exclusion + row_at >= col_at, 0.0, away)

    targets = jnp.int32(0)
    for offset in ORDER:
        targets += inside(position - offset).astype(jnp.int32)
    pl.semaphore_wait(barrier, targets)

    def copy(slot, offset):
        return pltpu.make_async_remote_copy(
            src_ref=series_ref,
            dst_ref=place(offset),
            send_sem=send_sem.at[slot],
            recv_sem=recv_sem.at[slot],
            device_id=device(position - offset),
            device_id_type=pl.DeviceIdType.MESH,
        )

    for slot, offset in enumerate(ORDER):

        @pl.when(inside(position - offset))
        def _():
            copy(slot, offset).start()

    local.wait()
    for slot, offset in enumerate(ORDER):

        @pl.when(inside(position + offset))
        def _():
            copy(slot, offset).wait_recv()

    mean, scale = window_stats(xs[...], length)
    mean_ref[...] = mean
    scale_ref[...] = scale

    def build(channel, z_ref):
        row = pl.ds(channel, 1)
        samples = jnp.broadcast_to(xs[row, :], (SUBLANES, width))
        for q in range(LANES // SUBLANES):
            left = LANES - 1 - SUBLANES * q
            shifted = pltpu.roll(samples, width - left, 1, stride=1, stride_axis=0)
            for tile in range(tiles):
                span = slice(tile * rows, tile * rows + rows)
                average = mean_ref[row, span]
                factor = scale_ref[row, span]
                parts = []
                for half in range(halves):
                    start = tile * rows + half * LANES
                    parts.append((shifted[:, start : start + rows] - average) * factor)
                group = SUBLANES * halves
                z_ref[tile, q * group : (q + 1) * group, :] = jnp.concatenate(
                    parts, axis=0
                ).astype(jnp.bfloat16)

    def match(channel, z_ref):
        own = z_ref[before].T
        best = None
        for tile in range(tiles):
            offset = tile - before
            if offset == 0:
                other = z_ref[before]
            else:
                spare = -2 * offset if abs(offset) == 1 else -offset
                index = jnp.where(inside(position + offset), tile, before + spare)
                other = z_ref[index]
            scores = jnp.dot(own, other, preferred_element_type=jnp.float32)
            if offset == 0:
                scores = scores + bias_ref[...]
            for start in range(0, rows, LANES):
                part = scores[:, start : start + LANES]
                if offset == 1 and start == 0:
                    edge = part[rows - exclusion :] + next_bias_ref[...]
                    part = jnp.concatenate([part[: rows - exclusion], edge], axis=0)
                if offset == -1 and start == rows - LANES:
                    edge = part[:exclusion] + prev_bias_ref[...]
                    part = jnp.concatenate([edge, part[exclusion:]], axis=0)
                best = part if best is None else jnp.maximum(best, part)
        top = jnp.max(best.T, axis=0, keepdims=True)
        out_ref[pl.ds(channel, 1), :] = jnp.sqrt(2.0 * length * (1.0 - top * (1.0 / length)))

    build(0, z_even)

    def pair(step, carry):
        first = 2 * step
        build(first + 1, z_odd)
        match(first, z_even)
        build(jnp.minimum(first + 2, channels - 1), z_even)
        match(first + 1, z_odd)
        return carry

    lax.fori_loop(0, channels // 2, pair, 0)

    for slot, offset in enumerate(ORDER):

        @pl.when(inside(position - offset))
        def _():
            copy(slot, offset).wait_send()


def shards(mesh, series, tail):
    channels, rows = series.shape
    length = tail.shape[1] + 1
    n_col = mesh.shape["col"]
    device_count = mesh.shape["band"] * n_col
    tiles = 2 * KD - 1
    width = 2 * KD * rows
    pairs = channels * tiles * rows * rows
    return pl.pallas_call(
        functools.partial(kernel, n_col, device_count),
        out_shape=jax.ShapeDtypeStruct((channels, rows), jnp.float32),
        in_specs=[
            pl.BlockSpec(memory_space=pl.ANY),
            pl.BlockSpec(memory_space=pltpu.VMEM),
        ],
        out_specs=pl.BlockSpec(memory_space=pltpu.VMEM),
        scratch_shapes=[
            pltpu.VMEM((channels, width), jnp.float32),
            pltpu.VMEM((channels, width), jnp.float32),
            pltpu.VMEM((channels, width), jnp.float32),
            pltpu.VMEM((rows, rows), jnp.float32),
            pltpu.VMEM((length // 4, LANES), jnp.float32),
            pltpu.VMEM((length // 4, LANES), jnp.float32),
            pltpu.VMEM((tiles, length, rows), jnp.bfloat16),
            pltpu.VMEM((tiles, length, rows), jnp.bfloat16),
            pltpu.SemaphoreType.DMA,
            pltpu.SemaphoreType.DMA((len(ORDER),)),
            pltpu.SemaphoreType.DMA((len(ORDER),)),
        ],
        compiler_params=pltpu.CompilerParams(
            collective_id=0, has_side_effects=True, vmem_limit_bytes=32 * 1024 * 1024
        ),
        cost_estimate=pl.CostEstimate(
            flops=2 * pairs * length, bytes_accessed=8 * channels * width, transcendentals=0
        ),
        name="profile_kernel",
    )(series, tail)


def solution(mesh):
    return jax.shard_map(
        functools.partial(shards, mesh),
        mesh=mesh,
        in_specs=(P(None, ("band", "col")), P()),
        out_specs=P(None, ("band", "col")),
        check_vma=False,
    )
```

```python
import functools

import jax
import jax.numpy as jnp
from jax import lax
from jax.experimental import pallas as pl
from jax.experimental.pallas import tpu as pltpu
from jax.sharding import PartitionSpec as P

KD = 4
LANES = 128
SUBLANES = 8

epsilon = 1e-06

ORDER = (1, 2, -1, 3, -2, 4, -3)


def window_stats(samples, length):
    width = samples.shape[1]
    mean, spread = samples, None
    count = 1
    while count < length:
        other = pltpu.roll(mean, width - count, 1)
        gap = mean - other
        term = gap * gap * (0.5 * count)
        if spread is None:
            spread = term
        else:
            spread = spread + pltpu.roll(spread, width - count, 1) + term
        mean = (mean + other) * 0.5
        count *= 2
    return mean, lax.rsqrt(spread * (1.0 / length) + epsilon)


def kernel(
    n_col,
    device_count,
    series_ref,
    tail_ref,
    out_ref,
    xs,
    mean_ref,
    scale_ref,
    bias_ref,
    next_bias_ref,
    prev_bias_ref,
    z_even,
    z_odd,
    own_even,
    own_odd,
    eye_ref,
    tail_buf,
    local_sem,
    tail_sem,
    send_sem,
    recv_sem,
):
    channels, rows = series_ref.shape
    length = tail_ref.shape[1] + 1
    halves = length // LANES
    exclusion = length // 4
    width = xs.shape[1]
    before = KD - 1
    tiles = 2 * KD - 1
    position = lax.axis_index("band") * n_col + lax.axis_index("col")

    def device(index):
        return {"band": index // n_col, "col": lax.rem(index, n_col)}

    def inside(index):
        return (index >= 0) & (index < device_count)

    barrier = pltpu.get_barrier_semaphore()
    for offset in ORDER:
        source = position + offset

        @pl.when(inside(source))
        def _():
            pl.semaphore_signal(
                barrier, inc=1, device_id=device(source), device_id_type=pl.DeviceIdType.MESH
            )

    def place(offset):
        return xs.at[:, pl.ds((before + offset) * rows, rows)]

    local = pltpu.make_async_copy(series_ref, place(0), local_sem)
    local.start()

    load_tail = pltpu.make_async_copy(tail_ref, tail_buf, tail_sem)
    load_tail.start()

    row_at = lax.broadcasted_iota(jnp.int32, (rows, rows), 0)
    col_at = lax.broadcasted_iota(jnp.int32, (rows, rows), 1)
    eye_ref[...] = jnp.where(row_at == col_at, 1.0, 0.0).astype(jnp.bfloat16)
    away = -16.0 * length
    bias_ref[...] = jnp.where(jnp.abs(row_at - col_at) >= exclusion, 0.0, away)
    row_at = lax.broadcasted_iota(jnp.int32, (exclusion, LANES), 0)
    col_at = lax.broadcasted_iota(jnp.int32, (exclusion, LANES), 1)
    next_bias_ref[...] = jnp.where(col_at >= row_at, 0.0, away)
    prev_bias_ref[...] = jnp.where(LANES - exclusion + row_at >= col_at, 0.0, away)

    targets = jnp.int32(0)
    for offset in ORDER:
        targets += inside(position - offset).astype(jnp.int32)
    pl.semaphore_wait(barrier, targets)

    def copy(slot, offset):
        return pltpu.make_async_remote_copy(
            src_ref=series_ref,
            dst_ref=place(offset),
            send_sem=send_sem.at[slot],
            recv_sem=recv_sem.at[slot],
            device_id=device(position - offset),
            device_id_type=pl.DeviceIdType.MESH,
        )

    for slot, offset in enumerate(ORDER):

        @pl.when(inside(position - offset))
        def _():
            copy(slot, offset).start()

    local.wait()
    load_tail.wait()
    for offset in range(1, KD + 1):

        @pl.when(position + offset == device_count)
        def _():
            start = (before + offset) * rows
            xs[:, start : start + length - 1] = tail_buf[...]

    for slot, offset in enumerate(ORDER):

        @pl.when(inside(position + offset))
        def _():
            copy(slot, offset).wait_recv()

    mean, scale = window_stats(xs[...], length)
    mean_ref[...] = mean
    scale_ref[...] = scale

    def build(channel, z_ref, own_ref):
        row = pl.ds(channel, 1)
        samples = jnp.broadcast_to(xs[row, :], (SUBLANES, width))
        staggered = pltpu.roll(samples, 0, 1, stride=1, stride_axis=0)
        for q in range(LANES // SUBLANES):
            left = LANES - 1 - SUBLANES * q
            shifted = pltpu.roll(staggered, width - left, 1)
            for tile in range(tiles):
                span = slice(tile * rows, tile * rows + rows)
                average = mean_ref[row, span]
                factor = scale_ref[row, span]
                parts = []
                for half in range(halves):
                    start = tile * rows + half * LANES
                    parts.append((shifted[:, start : start + rows] - average) * factor)
                group = SUBLANES * halves
                z_ref[tile, q * group : (q + 1) * group, :] = jnp.concatenate(
                    parts, axis=0
                ).astype(jnp.bfloat16)
        own_ref[...] = lax.dot_general(
            eye_ref[...],
            z_ref[before],
            (((1,), (1,)), ((), ())),
            preferred_element_type=jnp.float32,
        ).astype(jnp.bfloat16)

    def match(channel, z_ref, own_ref):
        own = own_ref[...]
        best = None
        for tile in range(tiles):
            offset = tile - before
            if offset == 0:
                other = z_ref[before]
            else:
                spare = -2 * offset if abs(offset) == 1 else -offset
                index = jnp.where(inside(position + offset), tile, before + spare)
                other = z_ref[index]
            scores = jnp.dot(own, other, preferred_element_type=jnp.float32)
            if offset == 0:
                scores = scores + bias_ref[...]
            for start in range(0, rows, LANES):
                part = scores[:, start : start + LANES]
                if offset == 1 and start == 0:
                    edge = part[rows - exclusion :] + next_bias_ref[...]
                    part = jnp.concatenate([part[: rows - exclusion], edge], axis=0)
                if offset == -1 and start == rows - LANES:
                    edge = part[:exclusion] + prev_bias_ref[...]
                    part = jnp.concatenate([edge, part[exclusion:]], axis=0)
                best = part if best is None else jnp.maximum(best, part)
        top = jnp.max(best.T, axis=0, keepdims=True)
        out_ref[pl.ds(channel, 1), :] = jnp.sqrt(2.0 * length * (1.0 - top * (1.0 / length)))

    even, odd = (z_even, own_even), (z_odd, own_odd)
    build(0, *even)

    def pair(step, carry):
        first = 2 * step
        build(first + 1, *odd)
        match(first, *even)
        build(first + 2, *even)
        match(first + 1, *odd)
        return carry

    lax.fori_loop(0, channels // 2 - 1, pair, 0)
    build(channels - 1, *odd)
    match(channels - 2, *even)
    match(channels - 1, *odd)

    for slot, offset in enumerate(ORDER):

        @pl.when(inside(position - offset))
        def _():
            copy(slot, offset).wait_send()


def shards(mesh, series, tail):
    channels, rows = series.shape
    length = tail.shape[1] + 1
    n_col = mesh.shape["col"]
    device_count = mesh.shape["band"] * n_col
    tiles = 2 * KD - 1
    width = 2 * KD * rows
    pairs = channels * tiles * rows * rows
    return pl.pallas_call(
        functools.partial(kernel, n_col, device_count),
        out_shape=jax.ShapeDtypeStruct((channels, rows), jnp.float32),
        in_specs=[
            pl.BlockSpec(memory_space=pltpu.HBM),
            pl.BlockSpec(memory_space=pltpu.HBM),
        ],
        out_specs=pl.BlockSpec(memory_space=pltpu.VMEM),
        scratch_shapes=[
            pltpu.VMEM((channels, width), jnp.float32),
            pltpu.VMEM((channels, width), jnp.float32),
            pltpu.VMEM((channels, width), jnp.float32),
            pltpu.VMEM((rows, rows), jnp.float32),
            pltpu.VMEM((length // 4, LANES), jnp.float32),
            pltpu.VMEM((length // 4, LANES), jnp.float32),
            pltpu.VMEM((tiles, length, rows), jnp.bfloat16),
            pltpu.VMEM((tiles, length, rows), jnp.bfloat16),
            pltpu.VMEM((rows, length), jnp.bfloat16),
            pltpu.VMEM((rows, length), jnp.bfloat16),
            pltpu.VMEM((rows, rows), jnp.bfloat16),
            pltpu.VMEM((channels, length - 1), jnp.float32),
            pltpu.SemaphoreType.DMA,
            pltpu.SemaphoreType.DMA,
            pltpu.SemaphoreType.DMA((len(ORDER),)),
            pltpu.SemaphoreType.DMA((len(ORDER),)),
        ],
        compiler_params=pltpu.CompilerParams(
            collective_id=0, has_side_effects=True, vmem_limit_bytes=63 * 1024 * 1024
        ),
        cost_estimate=pl.CostEstimate(
            flops=2 * pairs * length, bytes_accessed=8 * channels * width, transcendentals=0
        ),
        name="profile_kernel",
    )(series, tail)


def solution(mesh):
    return jax.shard_map(
        functools.partial(shards, mesh),
        mesh=mesh,
        in_specs=(P(None, ("band", "col")), P()),
        out_specs=P(None, ("band", "col")),
        check_vma=False,
    )
```

```python
import functools

import jax
import jax.numpy as jnp
from jax import lax
from jax.experimental import pallas as pl
from jax.experimental.pallas import tpu as pltpu
from jax.sharding import PartitionSpec as P

KD = 4
LANES = 128
SUBLANES = 8

epsilon = 1e-06

ORDER = (1, 2, -1, 3, -2, 4, -3)


def window_stats(samples, length):
    width = samples.shape[1]
    mean, spread = samples, None
    count = 1
    while count < length:
        other = pltpu.roll(mean, width - count, 1)
        gap = mean - other
        term = gap * gap * (0.5 * count)
        if spread is None:
            spread = term
        else:
            spread = spread + pltpu.roll(spread, width - count, 1) + term
        mean = (mean + other) * 0.5
        count *= 2
    return mean, lax.rsqrt(spread * (1.0 / length) + epsilon)


def kernel(
    n_col,
    device_count,
    series_ref,
    tail_ref,
    out_ref,
    xs,
    mean_ref,
    scale_ref,
    bias_ref,
    next_bias_ref,
    prev_bias_ref,
    z_even,
    z_odd,
    own_even,
    own_odd,
    eye_ref,
    tail_buf,
    local_sem,
    tail_sem,
    send_sem,
    recv_sem,
):
    channels, rows = series_ref.shape
    length = tail_ref.shape[1] + 1
    halves = length // LANES
    exclusion = length // 4
    width = xs.shape[1]
    before = KD - 1
    tiles = 2 * KD - 1
    position = lax.axis_index("band") * n_col + lax.axis_index("col")

    def device(index):
        return {"band": index // n_col, "col": lax.rem(index, n_col)}

    def inside(index):
        return (index >= 0) & (index < device_count)

    barrier = pltpu.get_barrier_semaphore()
    for offset in ORDER:
        source = position + offset

        @pl.when(inside(source))
        def _():
            pl.semaphore_signal(
                barrier, inc=1, device_id=device(source), device_id_type=pl.DeviceIdType.MESH
            )

    def place(offset):
        return xs.at[:, pl.ds((before + offset) * rows, rows)]

    local = pltpu.make_async_copy(series_ref, place(0), local_sem)
    local.start()

    load_tail = pltpu.make_async_copy(tail_ref, tail_buf, tail_sem)
    load_tail.start()

    row_at = lax.broadcasted_iota(jnp.int32, (rows, rows), 0)
    col_at = lax.broadcasted_iota(jnp.int32, (rows, rows), 1)
    eye_ref[...] = jnp.where(row_at == col_at, 1.0, 0.0).astype(jnp.bfloat16)
    away = -16.0 * length
    bias_ref[...] = jnp.where(jnp.abs(row_at - col_at) >= exclusion, 0.0, away)
    row_at = lax.broadcasted_iota(jnp.int32, (exclusion, LANES), 0)
    col_at = lax.broadcasted_iota(jnp.int32, (exclusion, LANES), 1)
    next_bias_ref[...] = jnp.where(col_at >= row_at, 0.0, away)
    prev_bias_ref[...] = jnp.where(LANES - exclusion + row_at >= col_at, 0.0, away)

    targets = jnp.int32(0)
    for offset in ORDER:
        targets += inside(position - offset).astype(jnp.int32)
    pl.semaphore_wait(barrier, targets)

    def copy(slot, offset):
        return pltpu.make_async_remote_copy(
            src_ref=series_ref,
            dst_ref=place(offset),
            send_sem=send_sem.at[slot],
            recv_sem=recv_sem.at[slot],
            device_id=device(position - offset),
            device_id_type=pl.DeviceIdType.MESH,
        )

    for slot, offset in enumerate(ORDER):

        @pl.when(inside(position - offset))
        def _():
            copy(slot, offset).start()

    local.wait()
    load_tail.wait()
    for offset in range(1, KD + 1):

        @pl.when(position + offset == device_count)
        def _():
            start = (before + offset) * rows
            xs[:, start : start + length - 1] = tail_buf[...]

    for slot, offset in enumerate(ORDER):

        @pl.when(inside(position + offset))
        def _():
            copy(slot, offset).wait_recv()

    mean, scale = window_stats(xs[...], length)
    mean_ref[...] = mean
    scale_ref[...] = scale

    def build(channel, z_ref, own_ref):
        row = pl.ds(channel, 1)
        samples = jnp.broadcast_to(xs[row, :], (SUBLANES, width))
        averages = jnp.broadcast_to(mean_ref[row, :], (SUBLANES, width))
        factors = jnp.broadcast_to(scale_ref[row, :], (SUBLANES, width))
        staggered = pltpu.roll(samples, 0, 1, stride=1, stride_axis=0)
        for q in range(LANES // SUBLANES):
            left = LANES - 1 - SUBLANES * q
            shifted = pltpu.roll(staggered, width - left, 1)
            for tile in range(tiles):
                span = slice(tile * rows, tile * rows + rows)
                average = averages[:, span]
                factor = factors[:, span]
                parts = []
                for half in range(halves):
                    start = tile * rows + half * LANES
                    parts.append((shifted[:, start : start + rows] - average) * factor)
                group = SUBLANES * halves
                z_ref[tile, q * group : (q + 1) * group, :] = jnp.concatenate(
                    parts, axis=0
                ).astype(jnp.bfloat16)
        own_ref[...] = lax.dot_general(
            eye_ref[...],
            z_ref[before],
            (((1,), (1,)), ((), ())),
            preferred_element_type=jnp.float32,
        ).astype(jnp.bfloat16)

    def match(channel, z_ref, own_ref):
        own = own_ref[...]
        best = None
        for tile in range(tiles):
            offset = tile - before
            if offset == 0:
                other = z_ref[before]
            else:
                spare = -2 * offset if abs(offset) == 1 else -offset
                index = jnp.where(inside(position + offset), tile, before + spare)
                other = z_ref[index]
            scores = jnp.dot(own, other, preferred_element_type=jnp.float32)
            if offset == 0:
                scores = scores + bias_ref[...]
            for start in range(0, rows, LANES):
                part = scores[:, start : start + LANES]
                if offset == 1 and start == 0:
                    edge = part[rows - exclusion :] + next_bias_ref[...]
                    part = jnp.concatenate([part[: rows - exclusion], edge], axis=0)
                if offset == -1 and start == rows - LANES:
                    edge = part[:exclusion] + prev_bias_ref[...]
                    part = jnp.concatenate([edge, part[exclusion:]], axis=0)
                best = part if best is None else jnp.maximum(best, part)
        top = jnp.max(best.T, axis=0, keepdims=True)
        out_ref[pl.ds(channel, 1), :] = jnp.sqrt(2.0 * length * (1.0 - top * (1.0 / length)))

    even, odd = (z_even, own_even), (z_odd, own_odd)
    build(0, *even)

    def pair(step, carry):
        first = 2 * step
        build(first + 1, *odd)
        match(first, *even)
        build(jnp.minimum(first + 2, channels - 1), *even)
        match(first + 1, *odd)
        return carry

    lax.fori_loop(0, channels // 2, pair, 0)

    for slot, offset in enumerate(ORDER):

        @pl.when(inside(position - offset))
        def _():
            copy(slot, offset).wait_send()


def shards(mesh, series, tail):
    channels, rows = series.shape
    length = tail.shape[1] + 1
    n_col = mesh.shape["col"]
    device_count = mesh.shape["band"] * n_col
    tiles = 2 * KD - 1
    width = 2 * KD * rows
    pairs = channels * tiles * rows * rows
    return pl.pallas_call(
        functools.partial(kernel, n_col, device_count),
        out_shape=jax.ShapeDtypeStruct((channels, rows), jnp.float32),
        in_specs=[
            pl.BlockSpec(memory_space=pltpu.HBM),
            pl.BlockSpec(memory_space=pltpu.HBM),
        ],
        out_specs=pl.BlockSpec(memory_space=pltpu.VMEM),
        scratch_shapes=[
            pltpu.VMEM((channels, width), jnp.float32),
            pltpu.VMEM((channels, width), jnp.float32),
            pltpu.VMEM((channels, width), jnp.float32),
            pltpu.VMEM((rows, rows), jnp.float32),
            pltpu.VMEM((length // 4, LANES), jnp.float32),
            pltpu.VMEM((length // 4, LANES), jnp.float32),
            pltpu.VMEM((tiles, length, rows), jnp.bfloat16),
            pltpu.VMEM((tiles, length, rows), jnp.bfloat16),
            pltpu.VMEM((rows, length), jnp.bfloat16),
            pltpu.VMEM((rows, length), jnp.bfloat16),
            pltpu.VMEM((rows, rows), jnp.bfloat16),
            pltpu.VMEM((channels, length - 1), jnp.float32),
            pltpu.SemaphoreType.DMA,
            pltpu.SemaphoreType.DMA,
            pltpu.SemaphoreType.DMA((len(ORDER),)),
            pltpu.SemaphoreType.DMA((len(ORDER),)),
        ],
        compiler_params=pltpu.CompilerParams(
            collective_id=0, has_side_effects=True, vmem_limit_bytes=32 * 1024 * 1024
        ),
        cost_estimate=pl.CostEstimate(
            flops=2 * pairs * length, bytes_accessed=8 * channels * width, transcendentals=0
        ),
        name="profile_kernel",
    )(series, tail)


def solution(mesh):
    return jax.shard_map(
        functools.partial(shards, mesh),
        mesh=mesh,
        in_specs=(P(None, ("band", "col")), P()),
        out_specs=P(None, ("band", "col")),
        check_vma=False,
    )
```

```python
import functools

import jax
import jax.numpy as jnp
from jax import lax
from jax.experimental import pallas as pl
from jax.experimental.pallas import tpu as pltpu
from jax.sharding import PartitionSpec as P

KD = 4
LANES = 128
SUBLANES = 8

epsilon = 1e-06

ORDER = (1, 2, -1, 3, -2, 4, -3)


def window_stats(samples, length):
    width = samples.shape[1]
    mean, spread = samples, None
    count = 1
    while count < length:
        other = pltpu.roll(mean, width - count, 1)
        gap = mean - other
        term = gap * gap * (0.5 * count)
        if spread is None:
            spread = term
        else:
            spread = spread + pltpu.roll(spread, width - count, 1) + term
        mean = (mean + other) * 0.5
        count *= 2
    return mean, lax.rsqrt(spread * (1.0 / length) + epsilon)


def kernel(
    n_col,
    device_count,
    series_ref,
    tail_ref,
    out_ref,
    xs,
    mean_ref,
    scale_ref,
    bias_ref,
    next_bias_ref,
    prev_bias_ref,
    z_even,
    z_odd,
    local_sem,
    send_sem,
    recv_sem,
):
    channels, rows = series_ref.shape
    length = tail_ref.shape[1] + 1
    halves = length // LANES
    exclusion = length // 4
    width = xs.shape[1]
    before = KD - 1
    tiles = 2 * KD - 1
    position = lax.axis_index("band") * n_col + lax.axis_index("col")

    def device(index):
        return {"band": index // n_col, "col": lax.rem(index, n_col)}

    def inside(index):
        return (index >= 0) & (index < device_count)

    barrier = pltpu.get_barrier_semaphore()
    for offset in ORDER:
        source = position + offset

        @pl.when(inside(source))
        def _():
            pl.semaphore_signal(
                barrier, inc=1, device_id=device(source), device_id_type=pl.DeviceIdType.MESH
            )

    def place(offset):
        return xs.at[:, pl.ds((before + offset) * rows, rows)]

    local = pltpu.make_async_copy(series_ref, place(0), local_sem)
    local.start()

    for offset in range(1, KD + 1):

        @pl.when(position + offset == device_count)
        def _():
            start = (before + offset) * rows
            xs[:, start : start + length - 1] = tail_ref[...]

    row_at = lax.broadcasted_iota(jnp.int32, (rows, rows), 0)
    col_at = lax.broadcasted_iota(jnp.int32, (rows, rows), 1)
    away = -16.0 * length
    bias_ref[...] = jnp.where(jnp.abs(row_at - col_at) >= exclusion, 0.0, away)
    row_at = lax.broadcasted_iota(jnp.int32, (exclusion, LANES), 0)
    col_at = lax.broadcasted_iota(jnp.int32, (exclusion, LANES), 1)
    next_bias_ref[...] = jnp.where(col_at >= row_at, 0.0, away)
    prev_bias_ref[...] = jnp.where(LANES - exclusion + row_at >= col_at, 0.0, away)

    targets = jnp.int32(0)
    for offset in ORDER:
        targets += inside(position - offset).astype(jnp.int32)
    pl.semaphore_wait(barrier, targets)

    def copy(slot, offset):
        return pltpu.make_async_remote_copy(
            src_ref=series_ref,
            dst_ref=place(offset),
            send_sem=send_sem.at[slot],
            recv_sem=recv_sem.at[slot],
            device_id=device(position - offset),
            device_id_type=pl.DeviceIdType.MESH,
        )

    for slot, offset in enumerate(ORDER):

        @pl.when(inside(position - offset))
        def _():
            copy(slot, offset).start()

    local.wait()
    for slot, offset in enumerate(ORDER):

        @pl.when(inside(position + offset))
        def _():
            copy(slot, offset).wait_recv()

    mean, scale = window_stats(xs[...], length)
    mean_ref[...] = mean
    scale_ref[...] = scale

    def build(channel, z_ref):
        row = pl.ds(channel, 1)
        samples = jnp.broadcast_to(xs[row, :], (SUBLANES, width))
        for q in range(LANES // SUBLANES):
            left = LANES - 1 - SUBLANES * q
            shifted = pltpu.roll(samples, width - left, 1, stride=1, stride_axis=0)
            for tile in range(tiles):
                span = slice(tile * rows, tile * rows + rows)
                average = mean_ref[row, span]
                factor = scale_ref[row, span]
                parts = []
                for half in range(halves):
                    start = tile * rows + half * LANES
                    parts.append((shifted[:, start : start + rows] - average) * factor)
                group = SUBLANES * halves
                z_ref[tile, q * group : (q + 1) * group, :] = jnp.concatenate(
                    parts, axis=0
                ).astype(jnp.bfloat16)

    order = list(range(tiles))
    groups = [order[:2], order[2:4], order[4:]]

    def match(channel, z_ref):
        own = z_ref[before].T
        best = None
        for group in groups:
            others = []
            for tile in group:
                offset = tile - before
                if offset == 0:
                    others.append(z_ref[before])
                    continue
                spare = -2 * offset if abs(offset) == 1 else -offset
                index = jnp.where(inside(position + offset), tile, before + spare)
                others.append(z_ref[index])
            product = jnp.dot(
                own, jnp.concatenate(others, axis=1), preferred_element_type=jnp.float32
            )
            for at, tile in enumerate(group):
                offset = tile - before
                scores = product[:, at * rows : (at + 1) * rows]
                if offset == 0:
                    scores = scores + bias_ref[...]
                for start in range(0, rows, LANES):
                    part = scores[:, start : start + LANES]
                    if offset == 1 and start == 0:
                        edge = part[rows - exclusion :] + next_bias_ref[...]
                        part = jnp.concatenate([part[: rows - exclusion], edge], axis=0)
                    if offset == -1 and start == rows - LANES:
                        edge = part[:exclusion] + prev_bias_ref[...]
                        part = jnp.concatenate([edge, part[exclusion:]], axis=0)
                    best = part if best is None else jnp.maximum(best, part)
        top = jnp.max(best.T, axis=0, keepdims=True)
        out_ref[pl.ds(channel, 1), :] = jnp.sqrt(2.0 * length * (1.0 - top * (1.0 / length)))

    build(0, z_even)

    def pair(step, carry):
        first = 2 * step
        build(first + 1, z_odd)
        match(first, z_even)
        build(jnp.minimum(first + 2, channels - 1), z_even)
        match(first + 1, z_odd)
        return carry

    lax.fori_loop(0, channels // 2, pair, 0)

    for slot, offset in enumerate(ORDER):

        @pl.when(inside(position - offset))
        def _():
            copy(slot, offset).wait_send()


def shards(mesh, series, tail):
    channels, rows = series.shape
    length = tail.shape[1] + 1
    n_col = mesh.shape["col"]
    device_count = mesh.shape["band"] * n_col
    tiles = 2 * KD - 1
    width = 2 * KD * rows
    pairs = channels * tiles * rows * rows
    return pl.pallas_call(
        functools.partial(kernel, n_col, device_count),
        out_shape=jax.ShapeDtypeStruct((channels, rows), jnp.float32),
        in_specs=[
            pl.BlockSpec(memory_space=pl.ANY),
            pl.BlockSpec(memory_space=pltpu.VMEM),
        ],
        out_specs=pl.BlockSpec(memory_space=pltpu.VMEM),
        scratch_shapes=[
            pltpu.VMEM((channels, width), jnp.float32),
            pltpu.VMEM((channels, width), jnp.float32),
            pltpu.VMEM((channels, width), jnp.float32),
            pltpu.VMEM((rows, rows), jnp.float32),
            pltpu.VMEM((length // 4, LANES), jnp.float32),
            pltpu.VMEM((length // 4, LANES), jnp.float32),
            pltpu.VMEM((tiles, length, rows), jnp.bfloat16),
            pltpu.VMEM((tiles, length, rows), jnp.bfloat16),
            pltpu.SemaphoreType.DMA,
            pltpu.SemaphoreType.DMA((len(ORDER),)),
            pltpu.SemaphoreType.DMA((len(ORDER),)),
        ],
        compiler_params=pltpu.CompilerParams(
            collective_id=0, has_side_effects=True, vmem_limit_bytes=32 * 1024 * 1024
        ),
        cost_estimate=pl.CostEstimate(
            flops=2 * pairs * length, bytes_accessed=8 * channels * width, transcendentals=0
        ),
        name="profile_kernel",
    )(series, tail)


def solution(mesh):
    return jax.shard_map(
        functools.partial(shards, mesh),
        mesh=mesh,
        in_specs=(P(None, ("band", "col")), P()),
        out_specs=P(None, ("band", "col")),
        check_vma=False,
    )
```

```python
import functools

import jax
import jax.numpy as jnp
from jax import lax
from jax.experimental import pallas as pl
from jax.experimental.pallas import tpu as pltpu
from jax.sharding import PartitionSpec as P

KD = 4
LANES = 128
SUBLANES = 8

epsilon = 1e-06

ORDER = (1, 2, -1, 3, -2, 4, -3)


def window_stats(samples, length):
    width = samples.shape[1]
    mean, spread = samples, None
    count = 1
    while count < length:
        other = pltpu.roll(mean, width - count, 1)
        gap = mean - other
        term = gap * gap * (0.5 * count)
        if spread is None:
            spread = term
        else:
            spread = spread + pltpu.roll(spread, width - count, 1) + term
        mean = (mean + other) * 0.5
        count *= 2
    return mean, lax.rsqrt(spread * (1.0 / length) + epsilon)


def kernel(
    n_col,
    device_count,
    series_ref,
    tail_ref,
    out_ref,
    xs,
    mean_ref,
    scale_ref,
    bias_ref,
    next_bias_ref,
    prev_bias_ref,
    z_ref,
    local_sem,
    send_sem,
    recv_sem,
):
    channels, rows = series_ref.shape
    length = tail_ref.shape[1] + 1
    halves = length // LANES
    exclusion = length // 4
    width = xs.shape[1]
    before = KD - 1
    tiles = 2 * KD - 1
    position = lax.axis_index("band") * n_col + lax.axis_index("col")

    def device(index):
        return {"band": index // n_col, "col": lax.rem(index, n_col)}

    def inside(index):
        return (index >= 0) & (index < device_count)

    barrier = pltpu.get_barrier_semaphore()
    for offset in ORDER:
        source = position + offset

        @pl.when(inside(source))
        def _():
            pl.semaphore_signal(
                barrier, inc=1, device_id=device(source), device_id_type=pl.DeviceIdType.MESH
            )

    def place(offset):
        return xs.at[:, pl.ds((before + offset) * rows, rows)]

    local = pltpu.make_async_copy(series_ref, place(0), local_sem)
    local.start()

    for offset in range(1, KD + 1):

        @pl.when(position + offset == device_count)
        def _():
            start = (before + offset) * rows
            xs[:, start : start + length - 1] = tail_ref[...]

    row_at = lax.broadcasted_iota(jnp.int32, (rows, rows), 0)
    col_at = lax.broadcasted_iota(jnp.int32, (rows, rows), 1)
    away = -16.0 * length
    bias_ref[...] = jnp.where(jnp.abs(row_at - col_at) >= exclusion, 0.0, away)
    row_at = lax.broadcasted_iota(jnp.int32, (exclusion, LANES), 0)
    col_at = lax.broadcasted_iota(jnp.int32, (exclusion, LANES), 1)
    next_bias_ref[...] = jnp.where(col_at >= row_at, 0.0, away)
    prev_bias_ref[...] = jnp.where(LANES - exclusion + row_at >= col_at, 0.0, away)

    targets = jnp.int32(0)
    for offset in ORDER:
        targets += inside(position - offset).astype(jnp.int32)
    pl.semaphore_wait(barrier, targets)

    def copy(slot, offset):
        return pltpu.make_async_remote_copy(
            src_ref=series_ref,
            dst_ref=place(offset),
            send_sem=send_sem.at[slot],
            recv_sem=recv_sem.at[slot],
            device_id=device(position - offset),
            device_id_type=pl.DeviceIdType.MESH,
        )

    for slot, offset in enumerate(ORDER):

        @pl.when(inside(position - offset))
        def _():
            copy(slot, offset).start()

    local.wait()
    for slot, offset in enumerate(ORDER):

        @pl.when(inside(position + offset))
        def _():
            copy(slot, offset).wait_recv()

    mean, scale = window_stats(xs[...], length)
    mean_ref[...] = mean
    scale_ref[...] = scale

    def build(channel):
        row = pl.ds(channel, 1)
        samples = jnp.broadcast_to(xs[row, :], (SUBLANES, width))
        for q in range(LANES // SUBLANES):
            left = LANES - 1 - SUBLANES * q
            shifted = pltpu.roll(samples, width - left, 1, stride=1, stride_axis=0)
            for tile in range(tiles):
                span = slice(tile * rows, tile * rows + rows)
                average = mean_ref[row, span]
                factor = scale_ref[row, span]
                parts = []
                for half in range(halves):
                    start = tile * rows + half * LANES
                    parts.append((shifted[:, start : start + rows] - average) * factor)
                group = SUBLANES * halves
                z_ref[tile, q * group : (q + 1) * group, :] = jnp.concatenate(
                    parts, axis=0
                ).astype(jnp.bfloat16)

    order = list(range(tiles))
    groups = [order[:2], order[2:4], order[4:]]

    def match(channel):
        own = z_ref[before].T
        best = None
        for group in groups:
            others = []
            for tile in group:
                offset = tile - before
                if offset == 0:
                    others.append(z_ref[before])
                    continue
                spare = -2 * offset if abs(offset) == 1 else -offset
                index = jnp.where(inside(position + offset), tile, before + spare)
                others.append(z_ref[index])
            product = jnp.dot(
                own, jnp.concatenate(others, axis=1), preferred_element_type=jnp.float32
            )
            for at, tile in enumerate(group):
                offset = tile - before
                scores = product[:, at * rows : (at + 1) * rows]
                if offset == 0:
                    scores = scores + bias_ref[...]
                for start in range(0, rows, LANES):
                    part = scores[:, start : start + LANES]
                    if offset == 1 and start == 0:
                        edge = part[rows - exclusion :] + next_bias_ref[...]
                        part = jnp.concatenate([part[: rows - exclusion], edge], axis=0)
                    if offset == -1 and start == rows - LANES:
                        edge = part[:exclusion] + prev_bias_ref[...]
                        part = jnp.concatenate([edge, part[exclusion:]], axis=0)
                    best = part if best is None else jnp.maximum(best, part)
        top = jnp.max(best.T, axis=0, keepdims=True)
        out_ref[pl.ds(channel, 1), :] = jnp.sqrt(2.0 * length * (1.0 - top * (1.0 / length)))

    def one(channel, carry):
        build(channel)
        match(channel)
        return carry

    lax.fori_loop(0, channels, one, 0)

    for slot, offset in enumerate(ORDER):

        @pl.when(inside(position - offset))
        def _():
            copy(slot, offset).wait_send()


def shards(mesh, series, tail):
    channels, rows = series.shape
    length = tail.shape[1] + 1
    n_col = mesh.shape["col"]
    device_count = mesh.shape["band"] * n_col
    tiles = 2 * KD - 1
    width = 2 * KD * rows
    pairs = channels * tiles * rows * rows
    return pl.pallas_call(
        functools.partial(kernel, n_col, device_count),
        out_shape=jax.ShapeDtypeStruct((channels, rows), jnp.float32),
        in_specs=[
            pl.BlockSpec(memory_space=pl.ANY),
            pl.BlockSpec(memory_space=pltpu.VMEM),
        ],
        out_specs=pl.BlockSpec(memory_space=pltpu.VMEM),
        scratch_shapes=[
            pltpu.VMEM((channels, width), jnp.float32),
            pltpu.VMEM((channels, width), jnp.float32),
            pltpu.VMEM((channels, width), jnp.float32),
            pltpu.VMEM((rows, rows), jnp.float32),
            pltpu.VMEM((length // 4, LANES), jnp.float32),
            pltpu.VMEM((length // 4, LANES), jnp.float32),
            pltpu.VMEM((tiles, length, rows), jnp.bfloat16),
            pltpu.SemaphoreType.DMA,
            pltpu.SemaphoreType.DMA((len(ORDER),)),
            pltpu.SemaphoreType.DMA((len(ORDER),)),
        ],
        compiler_params=pltpu.CompilerParams(
            collective_id=0, has_side_effects=True, vmem_limit_bytes=32 * 1024 * 1024
        ),
        cost_estimate=pl.CostEstimate(
            flops=2 * pairs * length, bytes_accessed=8 * channels * width, transcendentals=0
        ),
        name="profile_kernel",
    )(series, tail)


def solution(mesh):
    return jax.shard_map(
        functools.partial(shards, mesh),
        mesh=mesh,
        in_specs=(P(None, ("band", "col")), P()),
        out_specs=P(None, ("band", "col")),
        check_vma=False,
    )
```

```python
import functools

import jax
import jax.numpy as jnp
from jax import lax
from jax.experimental import pallas as pl
from jax.experimental.pallas import tpu as pltpu
from jax.sharding import PartitionSpec as P

KD = 4
LANES = 128
SUBLANES = 8

epsilon = 1e-06

ORDER = (1, 2, -1, 3, -2, 4, -3)


def window_stats(samples, length):
    width = samples.shape[1]
    mean, spread = samples, None
    count = 1
    while count < length:
        other = pltpu.roll(mean, width - count, 1)
        gap = mean - other
        term = gap * gap * (0.5 * count)
        if spread is None:
            spread = term
        else:
            spread = spread + pltpu.roll(spread, width - count, 1) + term
        mean = (mean + other) * 0.5
        count *= 2
    return mean, lax.rsqrt(spread * (1.0 / length) + epsilon)


def kernel(
    n_col,
    device_count,
    series_ref,
    tail_ref,
    out_ref,
    xs,
    mean_ref,
    scale_ref,
    bias_ref,
    next_bias_ref,
    prev_bias_ref,
    z_even,
    z_odd,
    local_sem,
    send_sem,
    recv_sem,
):
    channels, rows = series_ref.shape
    length = tail_ref.shape[1] + 1
    halves = length // LANES
    exclusion = length // 4
    width = xs.shape[1]
    before = KD - 1
    tiles = 2 * KD - 1
    position = lax.axis_index("band") * n_col + lax.axis_index("col")

    def device(index):
        return {"band": index // n_col, "col": lax.rem(index, n_col)}

    def inside(index):
        return (index >= 0) & (index < device_count)

    barrier = pltpu.get_barrier_semaphore()
    for offset in ORDER:
        source = position + offset

        @pl.when(inside(source))
        def _():
            pl.semaphore_signal(
                barrier, inc=1, device_id=device(source), device_id_type=pl.DeviceIdType.MESH
            )

    def place(offset):
        return xs.at[:, pl.ds((before + offset) * rows, rows)]

    local = pltpu.make_async_copy(series_ref, place(0), local_sem)
    local.start()

    for offset in range(1, KD + 1):

        @pl.when(position + offset == device_count)
        def _():
            start = (before + offset) * rows
            xs[:, start : start + length - 1] = tail_ref[...]

    row_at = lax.broadcasted_iota(jnp.int32, (rows, rows), 0)
    col_at = lax.broadcasted_iota(jnp.int32, (rows, rows), 1)
    away = -16.0 * length
    bias_ref[...] = jnp.where(jnp.abs(row_at - col_at) >= exclusion, 0.0, away)
    row_at = lax.broadcasted_iota(jnp.int32, (exclusion, LANES), 0)
    col_at = lax.broadcasted_iota(jnp.int32, (exclusion, LANES), 1)
    next_bias_ref[...] = jnp.where(col_at >= row_at, 0.0, away)
    prev_bias_ref[...] = jnp.where(LANES - exclusion + row_at >= col_at, 0.0, away)

    targets = jnp.int32(0)
    for offset in ORDER:
        targets += inside(position - offset).astype(jnp.int32)
    pl.semaphore_wait(barrier, targets)

    def copy(slot, offset):
        return pltpu.make_async_remote_copy(
            src_ref=series_ref,
            dst_ref=place(offset),
            send_sem=send_sem.at[slot],
            recv_sem=recv_sem.at[slot],
            device_id=device(position - offset),
            device_id_type=pl.DeviceIdType.MESH,
        )

    for slot, offset in enumerate(ORDER):

        @pl.when(inside(position - offset))
        def _():
            copy(slot, offset).start()

    local.wait()
    for slot, offset in enumerate(ORDER):

        @pl.when(inside(position + offset))
        def _():
            copy(slot, offset).wait_recv()

    mean, scale = window_stats(xs[...], length)
    mean_ref[...] = mean
    scale_ref[...] = scale

    def build(channel, z_ref):
        row = pl.ds(channel, 1)
        samples = jnp.broadcast_to(xs[row, :], (SUBLANES, width))
        for q in range(LANES // SUBLANES):
            left = LANES - 1 - SUBLANES * q
            shifted = pltpu.roll(samples, width - left, 1, stride=1, stride_axis=0)
            for tile in range(tiles):
                span = slice(tile * rows, tile * rows + rows)
                average = mean_ref[row, span]
                factor = scale_ref[row, span]
                parts = []
                for half in range(halves):
                    start = tile * rows + half * LANES
                    parts.append((shifted[:, start : start + rows] - average) * factor)
                group = SUBLANES * halves
                z_ref[tile, q * group : (q + 1) * group, :] = jnp.concatenate(
                    parts, axis=0
                ).astype(jnp.bfloat16)

    def match(channel, z_ref):
        own = z_ref[before].T
        best = None
        for tile in range(tiles):
            offset = tile - before
            if offset == 0:
                other = z_ref[before]
            else:
                spare = -2 * offset if abs(offset) == 1 else -offset
                index = jnp.where(inside(position + offset), tile, before + spare)
                other = z_ref[index]
            scores = jnp.dot(own, other, preferred_element_type=jnp.float32)
            if offset == 0:
                scores = scores + bias_ref[...]
            for start in range(0, rows, LANES):
                part = scores[:, start : start + LANES]
                if offset == 1 and start == 0:
                    edge = part[rows - exclusion :] + next_bias_ref[...]
                    part = jnp.concatenate([part[: rows - exclusion], edge], axis=0)
                if offset == -1 and start == rows - LANES:
                    edge = part[:exclusion] + prev_bias_ref[...]
                    part = jnp.concatenate([edge, part[exclusion:]], axis=0)
                best = part if best is None else jnp.maximum(best, part)
        top = jnp.max(best.T, axis=0, keepdims=True)
        out_ref[pl.ds(channel, 1), :] = jnp.sqrt(2.0 * length * (1.0 - top * (1.0 / length)))

    build(0, z_even)

    def pair(step, carry):
        first = 2 * step
        build(first + 1, z_odd)
        match(first, z_even)
        build(jnp.minimum(first + 2, channels - 1), z_even)
        match(first + 1, z_odd)
        return carry

    lax.fori_loop(0, channels // 2, pair, 0, unroll=2)

    for slot, offset in enumerate(ORDER):

        @pl.when(inside(position - offset))
        def _():
            copy(slot, offset).wait_send()


def shards(mesh, series, tail):
    channels, rows = series.shape
    length = tail.shape[1] + 1
    n_col = mesh.shape["col"]
    device_count = mesh.shape["band"] * n_col
    tiles = 2 * KD - 1
    width = 2 * KD * rows
    pairs = channels * tiles * rows * rows
    return pl.pallas_call(
        functools.partial(kernel, n_col, device_count),
        out_shape=jax.ShapeDtypeStruct((channels, rows), jnp.float32),
        in_specs=[
            pl.BlockSpec(memory_space=pl.ANY),
            pl.BlockSpec(memory_space=pltpu.VMEM),
        ],
        out_specs=pl.BlockSpec(memory_space=pltpu.VMEM),
        scratch_shapes=[
            pltpu.VMEM((channels, width), jnp.float32),
            pltpu.VMEM((channels, width), jnp.float32),
            pltpu.VMEM((channels, width), jnp.float32),
            pltpu.VMEM((rows, rows), jnp.float32),
            pltpu.VMEM((length // 4, LANES), jnp.float32),
            pltpu.VMEM((length // 4, LANES), jnp.float32),
            pltpu.VMEM((tiles, length, rows), jnp.bfloat16),
            pltpu.VMEM((tiles, length, rows), jnp.bfloat16),
            pltpu.SemaphoreType.DMA,
            pltpu.SemaphoreType.DMA((len(ORDER),)),
            pltpu.SemaphoreType.DMA((len(ORDER),)),
        ],
        compiler_params=pltpu.CompilerParams(
            collective_id=0, has_side_effects=True, vmem_limit_bytes=32 * 1024 * 1024
        ),
        cost_estimate=pl.CostEstimate(
            flops=2 * pairs * length, bytes_accessed=8 * channels * width, transcendentals=0
        ),
        name="profile_kernel",
    )(series, tail)


def solution(mesh):
    return jax.shard_map(
        functools.partial(shards, mesh),
        mesh=mesh,
        in_specs=(P(None, ("band", "col")), P()),
        out_specs=P(None, ("band", "col")),
        check_vma=False,
    )
```
